128 devices in a mesh: blk: 32 (over y, x, core), tok: 4 (over z).
Axes of the slice: x: 4, y: 4, z: 4, core: 2. Of those that a mesh axis runs over, the one named last changes fastest.
Arguments:
- tokens: bfloat16 [4096, 8192], P('tok', 'blk'), may hold values from -6 to 6
- w_first: bfloat16 [64, 128, 128], P('blk'), may hold values from -0.5 to 0.5
- w_second: bfloat16 [64, 8, 128, 128], P('blk'), may hold values from -0.1875 to 0.1875
- tile_src: int32 [64, 8], replicated, may hold values from 0 to 63, as said below
- tile_live: int32 [64, 8], replicated, may hold values 0 or 1
- grad_out: bfloat16 [4096, 8192], P('tok', 'blk'), may hold values from -6 to 6
Outputs:
- layer_out: bfloat16 [4096, 8192], P('tok', 'blk')
- grad_tokens: bfloat16 [4096, 8192], P('tok', 'blk')
- grad_first: float32 [64, 128, 128], P('blk', 'tok')
- grad_second: float32 [64, 8, 128, 128], P('blk', None, 'tok')
The draws below stay inside these ranges and needn't reach their ends.
Inputs may be any that keep to these rules, and one draw needn't show every extreme that they name: `tile_src`: for each d, the 16 entries of rows 2 * d to 2 * d + 1 name distinct blocks, and at most 1 of them lie in any one range of blocks 2 * s to 2 * s + 1; some range holds exactly 1 of them.
All inputs are finite; a program needn't handle non-finite values.
Results may differ from the reference program's by a relative error of at most 0.0049.
Values may be sent and summed in bfloat16 or wider, within the bound.
No kernel may reach another device: no remote copies, remote signals or barrier semaphores. Data moves between devices by JAX's collectives and lax.ppermute only.
A program may use at most 192 MiB of HBM per device.

```python
import jax
import jax.numpy as jnp
from jax import lax

NB = 64
BS = 128
K = 8
D = 8192
TOKENS = 4096
BPD = 2
N_BLK = 32


def draw_tile_src(key, part):
    key = jax.random.fold_in(key, 7)
    perm_key, shift_key = jax.random.split(key)
    orders = jax.vmap(lambda sub_key: jax.random.permutation(sub_key, N_BLK))(jax.random.split(perm_key, N_BLK))
    shifts = jax.random.randint(shift_key, (N_BLK, N_BLK), 0, BPD)
    slot_index = jnp.arange(BPD * K, dtype=jnp.int32)
    source_dev = orders[:, slot_index % N_BLK].astype(jnp.int32)
    offset = jnp.take_along_axis(shifts, source_dev, axis=1)
    within = (slot_index[None, :] // N_BLK + offset) % BPD
    return (source_dev * BPD + within).reshape(NB, K).astype(jnp.int32)


def plant(drawn, rng, smallest, high):
    longest = drawn.shape.index(max(drawn.shape))
    spots = []
    for shift in (0, 1):
        where = [jax.random.randint(jax.random.fold_in(rng, axis), (), 0, length) for axis, length in enumerate(drawn.shape)]
        where[longest] = (where[longest] + shift) % drawn.shape[longest]
        spots.append(tuple(where))
    return drawn.at[spots[0]].set(smallest).at[spots[1]].set(high)


def steps_of(own_key, dims, pieces, least, largest):
    loudness = 1.0
    for dim, shards_of in pieces:
        heights = jax.random.uniform(jax.random.fold_in(jax.random.fold_in(own_key, 6), dim), (shards_of,), jnp.float32, least / len(pieces), largest / len(pieces))
        loudness = loudness * jnp.repeat(jnp.exp(heights), dims[dim] // shards_of).reshape((-1,) + (1,) * (len(dims) - 1 - dim))
    return loudness


def scatter_about(own_key, dims, width, most, shards=(), held_as=jnp.bfloat16):
    gain = steps_of(own_key, dims, shards, -0.22, 0.18) if shards else 1.0
    values = jax.random.normal(own_key, dims, jnp.float32) * width * gain
    return jnp.minimum(jnp.maximum(values, -most), most).astype(held_as)


def setup_inputs(seed: int = 0) -> dict:
    key_list = jax.random.split(jax.random.key(seed), 7)
    tokens = scatter_about(key_list[0], (TOKENS, D), 1.0, 6.0, ((0, 4), (1, 32)))
    w_first = scatter_about(key_list[1], (NB, BS, BS), BS ** -0.5, 0.5, ((0, 32),))
    w_second = scatter_about(key_list[2], (NB, K, BS, BS), (K * BS) ** -0.5, 0.1875, ((0, 32),))
    tile_src = draw_tile_src(jax.random.fold_in(key_list[6], 71), 0)
    tile_live = plant((jax.random.randint(key_list[4], (NB, K), 0, 4) < 3).astype(jnp.int32), jax.random.fold_in(key_list[4], 1), 0, 1)
    grad_out = scatter_about(key_list[5], (TOKENS, D), 1.0, 6.0, ((0, 4), (1, 32)))
    return {"tokens": tokens, "w_first": w_first, "w_second": w_second, "tile_src": tile_src, "tile_live": tile_live, "grad_out": grad_out}


def reference(tokens, w_first, w_second, tile_src, tile_live, grad_out):
    tok_rows = tokens.shape[0]
    tok_blocks = tokens.reshape(tok_rows, NB, BS)
    pre_act = jnp.einsum('tnc,ncd->tnd', tok_blocks.astype(jnp.float32), w_first.astype(jnp.float32))
    activated = jax.nn.gelu(pre_act).astype(jnp.bfloat16)
    w_live = w_second * tile_live[:, :, None, None].astype(jnp.bfloat16)
    grad_blocks = grad_out.reshape(tok_rows, NB, BS)

    def forward_block(block_index):
        gathered = jnp.take(activated, tile_src[block_index], axis=1).astype(jnp.float32)
        tile_weights = w_live[block_index].astype(jnp.float32)
        grad_block = grad_blocks[:, block_index, :].astype(jnp.float32)
        product = jnp.einsum('tkc,kcd->td', gathered, tile_weights).astype(jnp.bfloat16)
        live_scale = tile_live[block_index].astype(jnp.float32)
        weight_grad = jnp.einsum('tkc,td->kcd', gathered, grad_block) * live_scale[:, None, None]
        return (product, weight_grad)
    products, grad_second = lax.map(forward_block, jnp.arange(NB, dtype=jnp.int32))
    layer_out = products.transpose(1, 0, 2).reshape(tok_rows, NB * BS)

    def backward_block(running, block_index):
        grad_block = grad_blocks[:, block_index, :].astype(jnp.float32)
        contribution = jnp.einsum('td,kcd->tkc', grad_block, w_live[block_index].astype(jnp.float32))
        return (running.at[:, tile_src[block_index], :].add(contribution), None)
    grad_act, _ = lax.scan(backward_block, jnp.zeros((tok_rows, NB, BS), jnp.float32), jnp.arange(NB, dtype=jnp.int32))
    _, gelu_pull = jax.vjp(jax.nn.gelu, pre_act)
    grad_pre = gelu_pull(grad_act)[0].astype(jnp.bfloat16)
    grad_tokens = jnp.einsum('tnd,ncd->tnc', grad_pre.astype(jnp.float32), w_first.astype(jnp.float32))
    grad_tokens = grad_tokens.astype(jnp.bfloat16).reshape(tok_rows, NB * BS)
    grad_first = jnp.einsum('tnc,tnd->ncd', tok_blocks.astype(jnp.float32), grad_pre.astype(jnp.float32))
    return (layer_out, grad_tokens, grad_first, grad_second)
```

```python
import functools

import jax
import jax.numpy as jnp
from jax import lax
from jax.experimental import pallas as pl
from jax.experimental.pallas import tpu as pltpu
from jax.sharding import PartitionSpec as P

NY, NX, NC, NZ = 4, 4, 2, 4
BF, F32 = jnp.bfloat16, jnp.float32
ROOT = 0.7978845608028654
CUBE = 0.044715
VMEM = pl.BlockSpec(memory_space=pltpu.VMEM)
SMEM = pl.BlockSpec(memory_space=pltpu.SMEM)
ANY = pl.BlockSpec(memory_space=pl.ANY)


def along(dy, dx, dc):
    pairs = []
    for y in range(NY):
        for x in range(NX):
            for c in range(NC):
                to = (((y + dy) % NY) * NX + (x + dx) % NX) * NC + (c + dc) % NC
                pairs.append(((y * NX + x) * NC + c, to))
    return pairs


def shift_y(value, step):
    return lax.ppermute(value, "blk", along(step, 0, 0))


def shift_x(value, step):
    return lax.ppermute(value, "blk", along(0, step, 0))


def swap_core(value):
    return lax.ppermute(value, "blk", along(0, 0, 1))


def shift_z(value, step):
    return lax.ppermute(value, "tok", [(z, (z + step) % NZ) for z in range(NZ)])


def dot(a, b, ca, cb):
    return lax.dot_general(a, b, (((ca,), (cb,)), ((), ())), preferred_element_type=F32)


def call(body, outs, in_specs, out_specs, flops, nbytes, scratch=()):
    return pl.pallas_call(
        body,
        out_shape=outs,
        in_specs=in_specs,
        out_specs=out_specs,
        scratch_shapes=list(scratch),
        compiler_params=pltpu.CompilerParams(vmem_limit_bytes=48 * 1024 * 1024),
        cost_estimate=pl.CostEstimate(flops=flops, bytes_accessed=nbytes, transcendentals=0),
    )


def sds(shape, dtype):
    return jax.ShapeDtypeStruct(shape, dtype)


def first_body(pos, tok, go, wf, a0, a1, a2, a3, g0, g1, g2, g3, slope):
    x = pos[1]
    for s, (a, g) in enumerate(((a0, g0), (a1, g1), (a2, g2), (a3, g3))):
        rows = pl.ds(pl.multiple_of(((x + s) & 3) * 256, 256), 256)
        g[...] = go[rows, :]
        for p in range(2):
            pre = dot(tok[rows, p * 128 : (p + 1) * 128], wf[p], 1, 0)
            sq = pre * pre
            th = jnp.tanh(ROOT * pre * (1.0 + CUBE * sq))
            a[p] = (0.5 * pre * (1.0 + th)).astype(BF)
            slope[s, p] = 0.5 * (1.0 + th) + 0.5 * pre * (1.0 - th * th) * (
                ROOT * (1.0 + 3.0 * CUBE * sq)
            )


def load_weights(pos, w_own, wq, buf, sems, base):
    z = pos[3]
    copies = [pltpu.make_async_copy(w_own, buf.at[0], sems.at[base])]
    for t, part in enumerate(wq):
        k0 = ((z - t) & 3) * 2
        for s in range(1, 4):
            copies.append(
                pltpu.make_async_copy(
                    part.at[s - 1], buf.at[s, :, pl.ds(k0, 2)], sems.at[base + 3 * t + s]
                )
            )
    return copies


def back_body(pos, src, live, w_own, q0, q1, q2, q3, g0, g1, g2, g3, s0, s1, s2, s3, own, wbuf, acc, sems):
    y, x, c = pos[0], pos[1], pos[2]
    copies = load_weights(pos, w_own, (q0, q1, q2, q3), wbuf, sems, 0)
    for copy in copies:
        copy.start()
    acc[...] = jnp.zeros_like(acc)
    for copy in copies:
        copy.wait()
    for s, g in enumerate((g0, g1, g2, g3)):
        for p in range(2):
            block = ((y * 4 + ((x - s) & 3)) * 2 + c) * 2 + p
            grad = g[:, p * 128 : (p + 1) * 128]
            for k in range(8):
                j = src[block, k]
                scale = live[block, k].astype(F32)
                r = j >> 1
                flat = (((r & 1) ^ c) * 16 + (((r >> 3) - y) & 3) * 4 + (((r >> 1) - x) & 3)) * 2 + (j & 1)
                acc[flat] += dot(grad, wbuf[s, p, k], 1, 1) * scale
    for s, out in enumerate((s0, s1, s2, s3)):
        out[...] = acc[32 + 8 * s : 40 + 8 * s].astype(BF)
    own[...] = acc[0:32]


def fore_body(pos, src, live, w_own, q0, q1, q2, q3, a0, a1, a2, a3, b0, b1, b2, b3, g0, g1, g2, g3,
              l0, l1, l2, l3, z0, z1, z2, z3, wbuf, abuf, cat, grads, sems):
    y, x, c, z = pos[0], pos[1], pos[2], pos[3]
    copies = load_weights(pos, w_own, (q0, q1, q2, q3), wbuf, sems, 0)
    for n, part in enumerate((a0, a1, a2, a3, b0, b1, b2, b3)):
        copies.append(pltpu.make_async_copy(part, abuf.at[n], sems.at[13 + n]))
    for copy in copies:
        copy.start()
    for copy in copies:
        copy.wait()
    for s, (g, out) in enumerate(((g0, l0), (g1, l1), (g2, l2), (g3, l3))):
        for p in range(2):
            n = s * 2 + p
            block = ((y * 4 + ((x - s) & 3)) * 2 + c) * 2 + p
            grad = g[:, p * 128 : (p + 1) * 128]
            for k in range(8):
                j = src[block, k]
                scale = live[block, k].astype(F32).astype(BF)
                r = j >> 1
                which = ((r & 1) ^ c) * 4 + ((y - (r >> 3)) & 3)
                cat[p, :, k * 128 : (k + 1) * 128] = abuf[which, (x - (r >> 1)) & 3, j & 1] * scale
            weights = wbuf[s, p].reshape(1024, 128)
            out[:, p * 128 : (p + 1) * 128] = dot(cat[p], weights, 1, 0).astype(BF)
            grads[...] = dot(cat[p], grad, 0, 0).reshape(8, 128, 128)
            z0[n] = grads[:, pl.ds(pl.multiple_of(z * 32, 32), 32), :]
            for t, to in ((1, z1), (2, z2), (3, z3)):
                rows = pl.ds(pl.multiple_of(((z + t) & 3) * 32, 32), 32)
                to[n] = grads[:, rows, :].astype(BF)


def last_body(pos, tok, wf, slope, h0, h1, h2, h3, gt, f0, f1, f2, f3, total):
    x, z = pos[1], pos[3]
    for s, h in enumerate((h0, h1, h2, h3)):
        rows = pl.ds(pl.multiple_of(((x - s) & 3) * 256, 256), 256)
        for p in range(2):
            cols = slice(p * 128, (p + 1) * 128)
            grad_pre = (h[p].astype(F32) * slope[(4 - s) % 4, p]).astype(BF)
            gt[rows, cols] = dot(grad_pre, wf[p], 1, 1).astype(BF)
            part = dot(tok[rows, cols], grad_pre, 0, 0)
            if s == 0:
                total[p] = part
            else:
                total[p] += part
    for t, out in enumerate((f0, f1, f2, f3)):
        out[...] = total[:, pl.ds(pl.multiple_of(((z + t) & 3) * 32, 32), 32), :]


def join_body(pos, p0, p1, p2, p3, out):
    x = pos[1]
    for s, part in enumerate((p0, p1, p2, p3)):
        out[pl.ds(pl.multiple_of(((x + s) & 3) * 256, 256), 256), :] = part[...]


def shards(tokens, w_first, w_second, tile_src, tile_live, grad_out):
    me, z = lax.axis_index("blk"), lax.axis_index("tok")
    pos = jnp.stack([me // 8, (me // 2) % 4, me % 2, z]).astype(jnp.int32)

    quarter = lax.dynamic_slice_in_dim(w_second, z * 2, 2, 1)
    q0 = jnp.stack([shift_x(quarter, s) for s in (1, 2, 3)])
    quarters = [q0] + [shift_z(q0, t) for t in (1, 2, 3)]

    chunk = sds((256, 256), BF)
    outs = call(
        first_body,
        [sds((2, 256, 128), BF)] * 4 + [chunk] * 4 + [sds((4, 2, 256, 128), F32)],
        [SMEM] + [VMEM] * 3,
        [VMEM] * 9,
        67_000_000 * 2,
        3_500_000,
    )(pos, tokens, grad_out, w_first)
    acts, grads, slope = outs[:4], outs[4:8], outs[8]
    act_row = jnp.stack([acts[0]] + [shift_x(acts[s], s) for s in (1, 2, 3)])
    grads = [grads[0]] + [shift_x(grads[s], s) for s in (1, 2, 3)]

    mine = [act_row] + [shift_y(act_row, s) for s in (1, 2, 3)]
    other = [swap_core(part) for part in mine]

    wscratch = pltpu.VMEM((4, 2, 8, 128, 128), BF)
    piece = sds((8, 256, 128), BF)
    outs = call(
        back_body,
        [piece] * 4 + [sds((32, 256, 128), F32)],
        [SMEM] * 3 + [ANY] * 5 + [VMEM] * 4,
        [VMEM] * 5,
        540_000_000 * 2,
        9_000_000,
        [wscratch, pltpu.VMEM((64, 256, 128), F32), pltpu.SemaphoreType.DMA((13,))],
    )(pos, tile_src, tile_live, w_second, *quarters, *grads)
    swapped = [swap_core(outs[s]) for s in (1, 2, 3, 0)]
    own = outs[4]
    sums = [own[8 * s : 8 * s + 8] + swapped[(s - 1) % 4].astype(F32) for s in range(4)]
    total = sums[0]
    for part in [shift_y(sums[s].astype(BF), s) for s in (1, 2, 3)]:
        total = total + part.astype(F32)
    pieces = [total[0:2]] + [
        shift_x(total[2 * s : 2 * s + 2].astype(BF), s) for s in (1, 2, 3)
    ]

    slab = (8, 8, 32, 128)
    outs = call(
        fore_body,
        [chunk] * 4 + [sds(slab, F32)] + [sds(slab, BF)] * 3,
        [SMEM] * 3 + [ANY] * 13 + [VMEM] * 4,
        [VMEM] * 8,
        2 * 540_000_000 * 2,
        12_000_000,
        [
            wscratch,
            pltpu.VMEM((8, 4, 2, 256, 128), BF),
            pltpu.VMEM((2, 256, 1024), BF),
            pltpu.VMEM((8, 128, 128), F32),
            pltpu.SemaphoreType.DMA((21,)),
        ],
    )(pos, tile_src, tile_live, w_second, *quarters, *mine, *other, *grads)
    rows = [outs[0]] + [shift_x(outs[s], -s) for s in (1, 2, 3)]
    layer_out = call(
        join_body, sds((1024, 256), BF), [SMEM] + [VMEM] * 4, VMEM, 0, 1_000_000
    )(pos, *rows)
    summed = outs[4]
    for part in [shift_z(outs[4 + t], t) for t in (1, 2, 3)]:
        summed = summed + part.astype(F32)
    grad_second = summed[0:2]
    for part in [shift_x(summed[2 * s : 2 * s + 2].astype(BF), -s) for s in (1, 2, 3)]:
        grad_second = grad_second + part.astype(F32)

    strip = sds((2, 32, 128), F32)
    outs = call(
        last_body,
        [sds((1024, 256), BF)] + [strip] * 4,
        [SMEM] + [VMEM] * 7,
        [VMEM] * 5,
        2 * 67_000_000 * 2,
        3_500_000,
        [pltpu.VMEM((2, 128, 128), F32)],
    )(pos, tokens, w_first, slope, *pieces)
    grad_tokens = outs[0]
    grad_first = outs[1]
    for part in [shift_z(outs[1 + t], t) for t in (1, 2, 3)]:
        grad_first = grad_first + part
    return (layer_out, grad_tokens, grad_first, grad_second)


def solution(mesh):
    in_specs = (
        P("tok", "blk"),
        P("blk", None, None),
        P("blk", None, None, None),
        P(),
        P(),
        P("tok", "blk"),
    )
    out_specs = (
        P("tok", "blk"),
        P("tok", "blk"),
        P("blk", "tok", None),
        P("blk", None, "tok", None),
    )
    return jax.shard_map(shards, mesh=mesh, in_specs=in_specs, out_specs=out_specs, check_vma=False)
```

```python
import functools

import jax
import jax.numpy as jnp
from jax import lax
from jax.experimental import pallas as pl
from jax.experimental.pallas import tpu as pltpu
from jax.sharding import PartitionSpec as P

NY, NX, NC, NZ = 4, 4, 2, 4
BF, F32 = jnp.bfloat16, jnp.float32
ROOT = 0.7978845608028654
CUBE = 0.044715
VMEM = pl.BlockSpec(memory_space=pltpu.VMEM)
SMEM = pl.BlockSpec(memory_space=pltpu.SMEM)
ANY = pl.BlockSpec(memory_space=pl.ANY)


def along(dy, dx, dc):
    pairs = []
    for y in range(NY):
        for x in range(NX):
            for c in range(NC):
                to = (((y + dy) % NY) * NX + (x + dx) % NX) * NC + (c + dc) % NC
                pairs.append(((y * NX + x) * NC + c, to))
    return pairs


def shift_y(value, step):
    return lax.ppermute(value, "blk", along(step, 0, 0))


def shift_x(value, step):
    return lax.ppermute(value, "blk", along(0, step, 0))


def swap_core(value):
    return lax.ppermute(value, "blk", along(0, 0, 1))


def shift_z(value, step):
    return lax.ppermute(value, "tok", [(z, (z + step) % NZ) for z in range(NZ)])


def dot(a, b, ca, cb):
    return lax.dot_general(a, b, (((ca,), (cb,)), ((), ())), preferred_element_type=F32)


def call(body, outs, in_specs, out_specs, flops, nbytes, mib, scratch=()):
    return pl.pallas_call(
        body,
        out_shape=outs,
        in_specs=in_specs,
        out_specs=out_specs,
        scratch_shapes=list(scratch),
        compiler_params=pltpu.CompilerParams(vmem_limit_bytes=mib * 1024 * 1024),
        cost_estimate=pl.CostEstimate(flops=flops, bytes_accessed=nbytes, transcendentals=0),
    )


def sds(shape, dtype):
    return jax.ShapeDtypeStruct(shape, dtype)


def first_body(pos, tok, go, wf, a0, a1, a2, a3, g0, g1, g2, g3, slope, tbuf, sems):
    x = pos[1]
    acts, grads = (a0, a1, a2, a3), (g0, g1, g2, g3)
    order = (1, 3, 2, 0)
    rows = [pl.ds(pl.multiple_of(((x + s) & 3) * 256, 256), 256) for s in range(4)]
    loads = {s: pltpu.make_async_copy(tok.at[rows[s]], tbuf.at[s], sems.at[s]) for s in order}
    moves = {s: pltpu.make_async_copy(go.at[rows[s]], grads[s], sems.at[4 + s]) for s in order}
    for s in order:
        loads[s].start()
    for s in order:
        moves[s].start()
    for s in order:
        loads[s].wait()
        for p in range(2):
            pre = dot(tbuf[s, :, p * 128 : (p + 1) * 128], wf[p], 1, 0)
            sq = pre * pre
            th = jnp.tanh(ROOT * pre * (1.0 + CUBE * sq))
            acts[s][p] = (0.5 * pre * (1.0 + th)).astype(BF)
            slope[s, p] = 0.5 * (1.0 + th) + 0.5 * pre * (1.0 - th * th) * (
                ROOT * (1.0 + 3.0 * CUBE * sq)
            )
    for s in order:
        moves[s].wait()


def tiles(s, p, z, w_own, w0, w1, w2a, w2b, w3):
    found = []
    for k in range(8):
        if s == 0:
            found.append((k, w_own, (p, k)))
        else:
            t, kk = k // 2, k % 2
            slot = ((z - t) & 3) * 2 + kk
            if t == 2:
                found.append((slot, (w2a, w2b)[p], (s - 1, kk)))
            else:
                found.append((slot, (w0, w1, None, w3)[t], (p, s - 1, kk)))
    return found


def back_body(pos, src, live, w_own, w0, w1, w2a, w2b, w3, g0, g1, g2, g3, s0, s1, s2, s3, own, acc):
    y, x, c, z = pos[0], pos[1], pos[2], pos[3]
    acc[...] = jnp.zeros_like(acc)
    for s, g in enumerate((g0, g1, g2, g3)):
        for p in range(2):
            block = ((y * 4 + ((x - s) & 3)) * 2 + c) * 2 + p
            grad = g[:, p * 128 : (p + 1) * 128]
            for slot, ref, at in tiles(s, p, z, w_own, w0, w1, w2a, w2b, w3):
                j = src[block, slot]
                scale = live[block, slot].astype(F32)
                r = j >> 1
                flat = (((r & 1) ^ c) * 16 + (((r >> 3) - y) & 3) * 4 + (((r >> 1) - x) & 3)) * 2 + (j & 1)
                acc[flat] += dot(grad, ref[at], 1, 1) * scale
    for s, out in enumerate((s0, s1, s2, s3)):
        out[...] = acc[32 + 8 * s : 40 + 8 * s].astype(BF)
    own[...] = acc[0:32]


def pick(cat, n, at, abuf, src, live, block, slot, y, x, c):
    j = src[block, slot]
    scale = live[block, slot].astype(F32).astype(BF)
    r = j >> 1
    which = ((r & 1) ^ c) * 4 + ((y - (r >> 3)) & 3)
    cat[n, :, at * 128 : (at + 1) * 128] = abuf[which, (x - (r >> 1)) & 3, j & 1] * scale


def weight_body(pos, src, live, abuf, g0, g1, g2, g3, z0, z1, z2, z3, cat, grads):
    y, x, c, z = pos[0], pos[1], pos[2], pos[3]
    for s, g in enumerate((g0, g1, g2, g3)):
        for p in range(2):
            n = s * 2 + p
            block = ((y * 4 + ((x - s) & 3)) * 2 + c) * 2 + p
            for k in range(8):
                pick(cat, p, k, abuf, src, live, block, k, y, x, c)
            grads[p] = dot(cat[p], g[:, p * 128 : (p + 1) * 128], 0, 0).reshape(8, 128, 128)
            for t, to in enumerate((z0, z1, z2, z3)):
                rows = pl.ds(pl.multiple_of(((z + t) & 3) * 32, 32), 32)
                to[n] = grads[p, :, rows, :].astype(to.dtype)


def layer_body(pos, src, live, w_own, w0, w1, w2a, w2b, w3, abuf, l0, l1, l2, l3, cat):
    y, x, c, z = pos[0], pos[1], pos[2], pos[3]
    for s, out in enumerate((l0, l1, l2, l3)):
        for p in range(2):
            block = ((y * 4 + ((x - s) & 3)) * 2 + c) * 2 + p
            found = tiles(s, p, z, w_own, w0, w1, w2a, w2b, w3)
            for k, (slot, _, _) in enumerate(found):
                pick(cat, p, k, abuf, src, live, block, slot, y, x, c)
            total = None
            for k in range(0, 8, 2):
                _, ref, at = found[k]
                pair = ref[at[:-1] + (slice(at[-1], at[-1] + 2),)].reshape(256, 128)
                part = dot(cat[p, :, k * 128 : (k + 2) * 128], pair, 1, 0)
                total = part if total is None else total + part
            out[:, p * 128 : (p + 1) * 128] = total.astype(BF)


def last_body(pos, tok, wf, slope, h0, h1, h2, h3, gt, f0, f1, f2, f3, total):
    x, z = pos[1], pos[3]
    for s, h in enumerate((h0, h1, h2, h3)):
        rows = pl.ds(pl.multiple_of(((x - s) & 3) * 256, 256), 256)
        for p in range(2):
            cols = slice(p * 128, (p + 1) * 128)
            grad_pre = (h[p].astype(F32) * slope[(4 - s) % 4, p]).astype(BF)
            gt[rows, cols] = dot(grad_pre, wf[p], 1, 1).astype(BF)
            part = dot(tok[rows, cols], grad_pre, 0, 0)
            if s == 0:
                total[p] = part
            else:
                total[p] += part
    for t, out in enumerate((f0, f1, f2, f3)):
        out[...] = total[:, pl.ds(pl.multiple_of(((z + t) & 3) * 32, 32), 32), :]


def join_body(pos, p0, p1, p2, p3, out):
    x = pos[1]
    for s, part in enumerate((p0, p1, p2, p3)):
        out[pl.ds(pl.multiple_of(((x + s) & 3) * 256, 256), 256), :] = part[...]


def ring_gather(value, shift):
    half = value.shape[0] // 2
    behind, ahead = shift(value, 1), shift(value, -1)
    return behind, ahead, shift(behind[:half], 1), shift(ahead[half:], -1)


def ring_sum(parts, shift):
    half = parts[2].shape[0] // 2
    low, high = shift(parts[2][:half], 1), shift(parts[2][half:], -1)
    one = jnp.concatenate([parts[1][:half] + low.astype(F32), parts[1][half:]]).astype(BF)
    three = jnp.concatenate([parts[3][:half], parts[3][half:] + high.astype(F32)]).astype(BF)
    return parts[0] + shift(one, 1).astype(F32) + shift(three, -1).astype(F32)


def shards(tokens, w_first, w_second, tile_src, tile_live, grad_out):
    me, z = lax.axis_index("blk"), lax.axis_index("tok")
    pos = jnp.stack([me // 8, (me // 2) % 4, me % 2, z]).astype(jnp.int32)

    quarter = lax.dynamic_slice_in_dim(w_second, z * 2, 2, 1)
    q0 = jnp.stack([shift_x(quarter, s) for s in (1, 2, 3)], axis=1)
    q1, q3, q2a, q2b = ring_gather(q0, shift_z)
    weights = (w_second, q0, q1, q2a[0], q2b[0], q3)

    chunk = sds((256, 256), BF)
    outs = call(
        first_body,
        [sds((2, 256, 128), BF)] * 4 + [chunk] * 4 + [sds((4, 2, 256, 128), F32)],
        [SMEM, ANY, ANY, VMEM],
        [VMEM] * 9,
        67_000_000 * 2,
        3_500_000,
        8,
        [pltpu.VMEM((4, 256, 256), BF), pltpu.SemaphoreType.DMA((8,))],
    )(pos, tokens, grad_out, w_first)
    acts, grads, slope = outs[:4], outs[4:8], outs[8]
    act_row = jnp.stack([acts[0]] + [shift_x(acts[s], s) for s in (1, 2, 3)])
    grads = [grads[0]] + [shift_x(grads[s], s) for s in (1, 2, 3)]

    behind, ahead, low, high = ring_gather(act_row, shift_y)
    mine = [act_row, behind, low, high, ahead]
    other = [swap_core(part) for part in mine]
    abuf = jnp.concatenate(mine + other).reshape(8, 4, 2, 256, 128)

    piece = sds((8, 256, 128), BF)
    outs = call(
        back_body,
        [piece] * 4 + [sds((32, 256, 128), F32)],
        [SMEM] * 3 + [VMEM] * 10,
        [VMEM] * 5,
        540_000_000 * 2,
        9_000_000,
        20,
        [pltpu.VMEM((64, 256, 128), F32)],
    )(pos, tile_src, tile_live, *weights, *grads)
    own = outs[4]
    swapped = {s: swap_core(outs[s]) for s in (2, 1, 3, 0)}
    sums = [own[8 * s : 8 * s + 8] + swapped[s].astype(F32) for s in range(4)]
    sums[2] = sums[2].astype(BF)
    total = ring_sum(sums, shift_y)
    pieces = [total[0:2]] + [
        shift_x(total[2 * s : 2 * s + 2].astype(BF), s) for s in (1, 2, 3)
    ]

    slab = (8, 8, 32, 128)
    cat = pltpu.VMEM((2, 256, 1024), BF)
    parts = call(
        weight_body,
        [sds(slab, F32), sds(slab, F32), sds(slab, BF), sds(slab, F32)],
        [SMEM] * 3 + [VMEM] * 5,
        [VMEM] * 4,
        540_000_000 * 2,
        12_000_000,
        14,
        [cat, pltpu.VMEM((2, 8, 128, 128), F32)],
    )(pos, tile_src, tile_live, abuf, *grads)
    summed = ring_sum(parts, shift_z)
    grad_second = summed[0:2]
    for part in [shift_x(summed[2 * s : 2 * s + 2].astype(BF), -s) for s in (1, 2, 3)]:
        grad_second = grad_second + part.astype(F32)

    outs = call(
        layer_body,
        [chunk] * 4,
        [SMEM] * 3 + [VMEM] * 7,
        [VMEM] * 4,
        540_000_000 * 2,
        9_000_000,
        10,
        [cat],
    )(pos, tile_src, tile_live, *weights, abuf)
    rows = [outs[0]] + [shift_x(outs[s], -s) for s in (1, 2, 3)]
    layer_out = call(
        join_body, sds((1024, 256), BF), [SMEM] + [VMEM] * 4, VMEM, 0, 1_000_000, 4
    )(pos, *rows)

    strip = sds((2, 32, 128), F32)
    outs = call(
        last_body,
        [sds((1024, 256), BF)] + [strip] * 4,
        [SMEM] + [VMEM] * 7,
        [VMEM] * 5,
        2 * 67_000_000 * 2,
        3_500_000,
        8,
        [pltpu.VMEM((2, 128, 128), F32)],
    )(pos, tokens, w_first, slope, *pieces)
    grad_tokens = outs[0]
    grad_first = outs[1]
    for part in [shift_z(outs[1 + t], t) for t in (1, 2, 3)]:
        grad_first = grad_first + part
    return (layer_out, grad_tokens, grad_first, grad_second)


def solution(mesh):
    in_specs = (
        P("tok", "blk"),
        P("blk", None, None),
        P("blk", None, None, None),
        P(),
        P(),
        P("tok", "blk"),
    )
    out_specs = (
        P("tok", "blk"),
        P("tok", "blk"),
        P("blk", "tok", None),
        P("blk", None, "tok", None),
    )
    return jax.shard_map(shards, mesh=mesh, in_specs=in_specs, out_specs=out_specs, check_vma=False)
```

```python
import functools

import jax
import jax.numpy as jnp
from jax import lax
from jax.experimental import pallas as pl
from jax.experimental.pallas import tpu as pltpu
from jax.sharding import PartitionSpec as P

NY, NX, NC, NZ = 4, 4, 2, 4
BF, F32 = jnp.bfloat16, jnp.float32
LIMIT = 56 * 1024 * 1024
ROOT = 0.7978845608028654
CUBE = 0.044715
def along(dy, dx, dc):
    pairs = []
    for y in range(NY):
        for x in range(NX):
            for c in range(NC):
                to = (((y + dy) % NY) * NX + (x + dx) % NX) * NC + (c + dc) % NC
                pairs.append(((y * NX + x) * NC + c, to))
    return pairs


def shift_x(value, step):
    return lax.ppermute(value, "blk", along(0, step, 0))


def swap_core(value):
    return lax.ppermute(value, "blk", along(0, 0, 1))


def shift_z(value, step):
    return lax.ppermute(value, "tok", [(z, (z + step) % NZ) for z in range(NZ)])


def dot(a, b, ca, cb):
    return lax.dot_general(a, b, (((ca,), (cb,)), ((), ())), preferred_element_type=F32)


def window(value):
    return pl.BlockSpec(value.shape, lambda step: (0,) * len(value.shape))


def call(body, outs, args, flops, nbytes, scratch=(), kept=()):
    specs = []
    for n, arg in enumerate(args):
        if arg.dtype == jnp.int32:
            specs.append(pl.BlockSpec(memory_space=pltpu.SMEM))
        elif n in kept:
            specs.append(pl.BlockSpec(memory_space=pl.ANY))
        else:
            specs.append(window(arg))
    return pl.pallas_call(
        lambda *refs: body(*refs),
        grid=(1,),
        out_shape=outs,
        in_specs=specs,
        out_specs=[window(out) for out in outs],
        scratch_shapes=list(scratch),
        compiler_params=pltpu.CompilerParams(vmem_limit_bytes=LIMIT),
        cost_estimate=pl.CostEstimate(flops=flops, bytes_accessed=nbytes, transcendentals=0),
    )(*args)


def sds(shape, dtype):
    return jax.ShapeDtypeStruct(shape, dtype)


def first_body(tok, wf, act, slope):
    for n in range(4):
        for p in range(2):
            pre = dot(tok[n * 256 : (n + 1) * 256, p * 128 : (p + 1) * 128], wf[p], 1, 0)
            sq = pre * pre
            th = jnp.tanh(ROOT * pre * (1.0 + CUBE * sq))
            out = (0.5 * pre * (1.0 + th)).astype(BF)
            for y in range(4):
                act[y * 4 + n, p] = out
            slope[n, p] = 0.5 * (1.0 + th) + 0.5 * pre * (1.0 - th * th) * (
                ROOT * (1.0 + 3.0 * CUBE * sq)
            )


def tiles(s, p, z, w_own, parts):
    found = []
    for t in range(4):
        for kk in range(2):
            rows = slice(kk * 128, (kk + 1) * 128)
            if s == 0:
                k = 2 * t + kk
                found.append((k, w_own, (p, slice(k * 128, (k + 1) * 128))))
            else:
                found.append((((z - t) & 3) * 2 + kk, parts[t], (s - 1, p, rows)))
    return found


def back_body(pos, src, live, *refs):
    away, own = refs[9:11]
    w_own, w0, w1, w2, w3, g0, g1, g2, g3 = refs[11:20]
    acc, sems = refs[20:]
    copies = [pltpu.make_async_copy(refs[n], refs[11 + n], sems.at[n]) for n in range(9)]
    for copy in copies:
        copy.start()
    y, x, c, z = pos[0], pos[1], pos[2], pos[3]
    acc[...] = jnp.zeros_like(acc)
    for copy in copies:
        copy.wait()
    for s, g in enumerate((g0, g1, g2, g3)):
        for p in range(2):
            block = ((y * 4 + ((x - s) & 3)) * 2 + c) * 2 + p
            grad = g[:, p * 128 : (p + 1) * 128]
            for slot, ref, at in tiles(s, p, z, w_own, (w0, w1, w2, w3)):
                j = src[block, slot]
                scale = live[block, slot].astype(F32)
                r = j >> 1
                acc[((r & 1) ^ c) * 32 + (r >> 1) * 2 + (j & 1)] += dot(grad, ref[at], 1, 1) * scale
    for n in range(16):
        away[n] = acc[32 + 2 * n : 34 + 2 * n].astype(BF)
        own[n] = acc[2 * n : 2 * n + 2].astype(BF)


def load_acts(mine, other, abuf, sems):
    copies = [
        pltpu.make_async_copy(part, abuf.at[n], sems.at[n]) for n, part in enumerate((mine, other))
    ]
    for copy in copies:
        copy.start()
    for copy in copies:
        copy.wait()


def pick(cat, n, at, abuf, src, live, block, slot, c):
    j = src[block, slot]
    scale = live[block, slot].astype(F32).astype(BF)
    r = j >> 1
    cat[n, :, at * 128 : (at + 1) * 128] = abuf[(r & 1) ^ c, r >> 1, j & 1] * scale


def weight_body(pos, src, live, mine, other, g0, g1, g2, g3, z0, z1, z2, z3, abuf, cat, grads, sems):
    y, x, c, z = pos[0], pos[1], pos[2], pos[3]
    load_acts(mine, other, abuf, sems)
    for s, g in enumerate((g0, g1, g2, g3)):
        for p in range(2):
            n = s * 2 + p
            block = ((y * 4 + ((x - s) & 3)) * 2 + c) * 2 + p
            for k in range(8):
                pick(cat, p, k, abuf, src, live, block, k, c)
            grads[p] = dot(cat[p], g[:, p * 128 : (p + 1) * 128], 0, 0).reshape(8, 128, 128)
            for t, to in enumerate((z0, z1, z2, z3)):
                rows = pl.ds(pl.multiple_of(((z + t) & 3) * 32, 32), 32)
                to[n] = grads[p, :, rows, :].astype(to.dtype)


def layer_body(pos, src, live, w_own, w0, w1, w2, w3, mine, other, l0, l1, l2, l3, abuf, cat, sems):
    y, x, c, z = pos[0], pos[1], pos[2], pos[3]
    load_acts(mine, other, abuf, sems)
    for s, out in enumerate((l0, l1, l2, l3)):
        for p in range(2):
            block = ((y * 4 + ((x - s) & 3)) * 2 + c) * 2 + p
            found = tiles(s, p, z, w_own, (w0, w1, w2, w3))
            for k, (slot, _, _) in enumerate(found):
                pick(cat, p, k, abuf, src, live, block, slot, c)
            total = None
            for k in range(0, 8, 2):
                _, ref, at = found[k]
                both = ref[at[:-1] + (slice(at[-1].start, at[-1].start + 256),)]
                part = dot(cat[p, :, k * 128 : (k + 2) * 128], both, 1, 0)
                total = part if total is None else total + part
            out[:, p * 128 : (p + 1) * 128] = total.astype(BF)


def join_body(pos, p0, p1, p2, p3, out):
    x = pos[1]
    for s, part in enumerate((p0, p1, p2, p3)):
        out[pl.ds(pl.multiple_of(((x + s) & 3) * 256, 256), 256), :] = part[...]


def last_body(pos, tok, wf, slope, sums, gt, f0, f1, f2, f3, total):
    z = pos[3]
    for n in range(4):
        rows = slice(n * 256, (n + 1) * 256)
        for p in range(2):
            cols = slice(p * 128, (p + 1) * 128)
            grad_act = sums[n, p].astype(F32)
            for y in range(1, 4):
                grad_act += sums[y * 4 + n, p].astype(F32)
            grad_pre = (grad_act * slope[n, p]).astype(BF)
            gt[rows, cols] = dot(grad_pre, wf[p], 1, 1).astype(BF)
            part = dot(tok[rows, cols], grad_pre, 0, 0)
            if n == 0:
                total[p] = part
            else:
                total[p] += part
    for t, out in enumerate((f0, f1, f2, f3)):
        out[...] = total[:, pl.ds(pl.multiple_of(((z + t) & 3) * 32, 32), 32), :]


def exchange(value):
    groups = [[n * NC + c for n in range(NY * NX)] for c in range(NC)]
    return lax.all_to_all(value, "blk", 0, 0, axis_index_groups=groups, tiled=True)


def shards(tokens, w_first, w_second, tile_src, tile_live, grad_out):
    me, z = lax.axis_index("blk"), lax.axis_index("tok")
    pos = jnp.stack([me // 8, (me // 2) % 4, me % 2, z]).astype(jnp.int32)
    w_own = w_second.reshape(2, 1024, 128)

    quarter = lax.dynamic_slice_in_dim(w_own, z * 256, 256, 1)
    w0 = jnp.stack([shift_x(quarter, s) for s in (1, 2, 3)])

    whole, chunk = (16, 2, 256, 128), sds((256, 256), BF)
    x = (me // 2) % 4
    grads = [
        lax.dynamic_slice_in_dim(grad_out, ((x + s) % 4) * 256, 256, 0) for s in range(4)
    ]
    grads = [grads[0]] + [shift_x(grads[s], s) for s in (1, 2, 3)]
    act, slope = call(
        first_body,
        [sds(whole, BF), sds((4, 2, 256, 128), F32)],
        [tokens, w_first],
        67_000_000 * 2,
        3_500_000,
    )
    act, *_ = lax.optimization_barrier((act, w0, *grads[1:]))
    mine = exchange(act)
    weights = [w_own, w0] + [shift_z(w0, t) for t in (1, 2, 3)]

    inputs = [*weights, *grads]
    away, own = pl.pallas_call(
        back_body,
        out_shape=[sds(whole, BF)] * 2,
        in_specs=[pl.BlockSpec(memory_space=pltpu.SMEM)] * 3 + [pl.BlockSpec(memory_space=pl.ANY)] * 9,
        out_specs=[pl.BlockSpec(memory_space=pltpu.VMEM)] * 2,
        scratch_shapes=[pltpu.VMEM(part.shape, BF) for part in inputs]
        + [pltpu.VMEM((64, 256, 128), F32), pltpu.SemaphoreType.DMA((9,))],
        compiler_params=pltpu.CompilerParams(vmem_limit_bytes=LIMIT),
        cost_estimate=pl.CostEstimate(flops=1_080_000_000, bytes_accessed=9_000_000, transcendentals=0),
    )(pos, tile_src, tile_live, *inputs)
    away, mine = lax.optimization_barrier((away, mine))
    parts = (own.astype(F32) + swap_core(away).astype(F32)).astype(BF)
    parts, mine_later = lax.optimization_barrier((parts, mine))
    sums = exchange(parts)
    other = swap_core(mine_later)

    slab = (8, 8, 32, 128)
    cat = pltpu.VMEM((2, 256, 1024), BF)
    abuf = pltpu.VMEM((2, 16, 2, 256, 128), BF)
    parts = call(
        weight_body,
        [sds(slab, F32)] + [sds(slab, BF)] * 3,
        [pos, tile_src, tile_live, mine, other, *grads],
        540_000_000 * 2,
        12_000_000,
        [abuf, cat, pltpu.VMEM((2, 8, 128, 128), F32), pltpu.SemaphoreType.DMA((2,))],
        (3, 4),
    )
    summed, after_z = parts[0], [shift_z(parts[t], t) for t in (1, 2, 3)]
    other, _ = lax.optimization_barrier((other, parts[1]))
    layer = call(
        layer_body,
        [chunk] * 4,
        [pos, tile_src, tile_live, *weights, mine, other],
        540_000_000 * 2,
        9_000_000,
        [abuf, cat, pltpu.SemaphoreType.DMA((2,))],
        (8, 9),
    )
    sums, *_ = lax.optimization_barrier((sums, *layer))
    outs = call(
        last_body,
        [sds((1024, 256), BF)] + [sds((2, 32, 128), F32)] * 4,
        [pos, tokens, w_first, slope, sums],
        2 * 67_000_000 * 2,
        3_500_000,
        [pltpu.VMEM((2, 128, 128), F32)],
    )
    grad_tokens = outs[0]
    grad_first = outs[1]
    for part in [shift_z(outs[1 + t], t) for t in (1, 2, 3)]:
        grad_first = grad_first + part
    for part in after_z:
        summed = summed + part.astype(F32)
    grad_second = summed[0:2]
    for part in [shift_x(summed[2 * s : 2 * s + 2].astype(BF), -s) for s in (1, 2, 3)]:
        grad_second = grad_second + part.astype(F32)

    rows = [layer[0], shift_x(layer[1], -1), None, shift_x(layer[3], -3)]
    layer2, _ = lax.optimization_barrier((layer[2], rows[1]))
    rows[2] = shift_x(layer2, -2)
    (layer_out,) = call(join_body, [sds((1024, 256), BF)], [pos, *rows], 0, 1_000_000)
    return (layer_out, grad_tokens, grad_first, grad_second)


def solution(mesh):
    in_specs = (
        P("tok", "blk"),
        P("blk", None, None),
        P("blk", None, None, None),
        P(),
        P(),
        P("tok", "blk"),
    )
    out_specs = (
        P("tok", "blk"),
        P("tok", "blk"),
        P("blk", "tok", None),
        P("blk", None, "tok", None),
    )
    return jax.shard_map(shards, mesh=mesh, in_specs=in_specs, out_specs=out_specs, check_vma=False)
```

```python
import functools

import jax
import jax.numpy as jnp
from jax import lax
from jax.experimental import pallas as pl
from jax.experimental.pallas import tpu as pltpu
from jax.sharding import PartitionSpec as P

NY, NX, NC, NZ = 4, 4, 2, 4
BF, F32 = jnp.bfloat16, jnp.float32
LIMIT = 56 * 1024 * 1024
ROOT = 0.7978845608028654
CUBE = 0.044715
def along(dy, dx, dc):
    pairs = []
    for y in range(NY):
        for x in range(NX):
            for c in range(NC):
                to = (((y + dy) % NY) * NX + (x + dx) % NX) * NC + (c + dc) % NC
                pairs.append(((y * NX + x) * NC + c, to))
    return pairs


def shift_x(value, step):
    return lax.ppermute(value, "blk", along(0, step, 0))


def swap_core(value):
    return lax.ppermute(value, "blk", along(0, 0, 1))


def shift_z(value, step):
    return lax.ppermute(value, "tok", [(z, (z + step) % NZ) for z in range(NZ)])


def dot(a, b, ca, cb):
    return lax.dot_general(a, b, (((ca,), (cb,)), ((), ())), preferred_element_type=F32)


def window(value):
    return pl.BlockSpec(value.shape, lambda step: (0,) * len(value.shape))


def call(body, outs, args, flops, nbytes, scratch=(), kept=()):
    specs = []
    for n, arg in enumerate(args):
        if arg.dtype == jnp.int32:
            specs.append(pl.BlockSpec(memory_space=pltpu.SMEM))
        elif n in kept:
            specs.append(pl.BlockSpec(memory_space=pl.ANY))
        else:
            specs.append(window(arg))
    return pl.pallas_call(
        lambda *refs: body(*refs),
        grid=(1,),
        out_shape=outs,
        in_specs=specs,
        out_specs=[window(out) for out in outs],
        scratch_shapes=list(scratch),
        compiler_params=pltpu.CompilerParams(vmem_limit_bytes=LIMIT),
        cost_estimate=pl.CostEstimate(flops=flops, bytes_accessed=nbytes, transcendentals=0),
    )(*args)


def sds(shape, dtype):
    return jax.ShapeDtypeStruct(shape, dtype)


def first_body(tok, wf, act, slope):
    for n in range(4):
        for p in range(2):
            pre = dot(tok[n * 256 : (n + 1) * 256, p * 128 : (p + 1) * 128], wf[p], 1, 0)
            sq = pre * pre
            th = jnp.tanh(ROOT * pre * (1.0 + CUBE * sq))
            out = (0.5 * pre * (1.0 + th)).astype(BF)
            for y in range(4):
                act[y * 4 + n, p] = out
            slope[n, p] = 0.5 * (1.0 + th) + 0.5 * pre * (1.0 - th * th) * (
                ROOT * (1.0 + 3.0 * CUBE * sq)
            )


def tiles(s, p, z, w_own, parts):
    found = []
    for t in range(4):
        for kk in range(2):
            rows = slice(kk * 128, (kk + 1) * 128)
            if s == 0:
                k = 2 * t + kk
                found.append((k, w_own, (p, slice(k * 128, (k + 1) * 128))))
            else:
                found.append((((z - t) & 3) * 2 + kk, parts[t], (s - 1, p, rows)))
    return found


def back_body(pos, src, live, *refs):
    away, own = refs[9:11]
    w_own, w0, w1, w2, w3, g0, g1, g2, g3 = refs[11:20]
    acc, sems = refs[20:]
    copies = [pltpu.make_async_copy(refs[n], refs[11 + n], sems.at[n]) for n in range(9)]
    for n in (0, 5, 1, 2, 3, 4, 6, 7, 8):
        copies[n].start()
    y, x, c, z = pos[0], pos[1], pos[2], pos[3]
    acc[...] = jnp.zeros_like(acc)
    for s, g in enumerate((g0, g1, g2, g3)):
        for n in ((0, 5), (1, 2, 3, 4, 6), (7,), (8,))[s]:
            copies[n].wait()
        for p in range(2):
            block = ((y * 4 + ((x - s) & 3)) * 2 + c) * 2 + p
            grad = g[:, p * 128 : (p + 1) * 128]
            for slot, ref, at in tiles(s, p, z, w_own, (w0, w1, w2, w3)):
                j = src[block, slot]
                scale = live[block, slot].astype(F32)
                r = j >> 1
                acc[((r & 1) ^ c) * 32 + (r >> 1) * 2 + (j & 1)] += dot(grad, ref[at], 1, 1) * scale
    for n in range(16):
        away[n] = acc[32 + 2 * n : 34 + 2 * n].astype(BF)
        own[n] = acc[2 * n : 2 * n + 2].astype(BF)


def load_acts(mine, other, abuf, sems):
    copies = [
        pltpu.make_async_copy(part, abuf.at[n], sems.at[n]) for n, part in enumerate((mine, other))
    ]
    for copy in copies:
        copy.start()
    for copy in copies:
        copy.wait()


def pick(cat, n, at, abuf, src, live, block, slot, c):
    j = src[block, slot]
    scale = live[block, slot].astype(F32).astype(BF)
    r = j >> 1
    cat[n, :, at * 128 : (at + 1) * 128] = abuf[(r & 1) ^ c, r >> 1, j & 1] * scale


def weight_body(pos, src, live, mine, other, g0, g1, g2, g3, z0, z1, z2, z3, abuf, cat, grads, sems):
    y, x, c, z = pos[0], pos[1], pos[2], pos[3]
    load_acts(mine, other, abuf, sems)
    for s, g in enumerate((g0, g1, g2, g3)):
        for p in range(2):
            n = s * 2 + p
            block = ((y * 4 + ((x - s) & 3)) * 2 + c) * 2 + p
            for k in range(8):
                pick(cat, p, k, abuf, src, live, block, k, c)
            grads[p] = dot(cat[p], g[:, p * 128 : (p + 1) * 128], 0, 0).reshape(8, 128, 128)
            for t, to in enumerate((z0, z1, z2, z3)):
                rows = pl.ds(pl.multiple_of(((z + t) & 3) * 32, 32), 32)
                to[n] = grads[p, :, rows, :].astype(to.dtype)


def layer_body(pos, src, live, w_own, w0, w1, w2, w3, mine, other, l0, l1, l2, l3, abuf, cat, sems):
    y, x, c, z = pos[0], pos[1], pos[2], pos[3]
    load_acts(mine, other, abuf, sems)
    for s, out in enumerate((l0, l1, l2, l3)):
        for p in range(2):
            block = ((y * 4 + ((x - s) & 3)) * 2 + c) * 2 + p
            found = tiles(s, p, z, w_own, (w0, w1, w2, w3))
            for k, (slot, _, _) in enumerate(found):
                pick(cat, p, k, abuf, src, live, block, slot, c)
            total = None
            for k in range(0, 8, 2):
                _, ref, at = found[k]
                both = ref[at[:-1] + (slice(at[-1].start, at[-1].start + 256),)]
                part = dot(cat[p, :, k * 128 : (k + 2) * 128], both, 1, 0)
                total = part if total is None else total + part
            out[:, p * 128 : (p + 1) * 128] = total.astype(BF)


def join_body(pos, p0, p1, p2, p3, out):
    x = pos[1]
    for s, part in enumerate((p0, p1, p2, p3)):
        out[pl.ds(pl.multiple_of(((x + s) & 3) * 256, 256), 256), :] = part[...]


def last_body(pos, tok, wf, slope, sums, gt, f0, f1, f2, f3, total):
    z = pos[3]
    for n in range(4):
        rows = slice(n * 256, (n + 1) * 256)
        for p in range(2):
            cols = slice(p * 128, (p + 1) * 128)
            grad_act = sums[n, p].astype(F32)
            for y in range(1, 4):
                grad_act += sums[y * 4 + n, p].astype(F32)
            grad_pre = (grad_act * slope[n, p]).astype(BF)
            gt[rows, cols] = dot(grad_pre, wf[p], 1, 1).astype(BF)
            part = dot(tok[rows, cols], grad_pre, 0, 0)
            if n == 0:
                total[p] = part
            else:
                total[p] += part
    for t, out in enumerate((f0, f1, f2, f3)):
        out[...] = total[:, pl.ds(pl.multiple_of(((z + t) & 3) * 32, 32), 32), :]


def exchange(value):
    groups = [[n * NC + c for n in range(NY * NX)] for c in range(NC)]
    return lax.all_to_all(value, "blk", 0, 0, axis_index_groups=groups, tiled=True)


def shards(tokens, w_first, w_second, tile_src, tile_live, grad_out):
    me, z = lax.axis_index("blk"), lax.axis_index("tok")
    pos = jnp.stack([me // 8, (me // 2) % 4, me % 2, z]).astype(jnp.int32)
    w_own = w_second.reshape(2, 1024, 128)

    quarter = lax.dynamic_slice_in_dim(w_own, z * 256, 256, 1)
    w0 = jnp.stack([shift_x(quarter, s) for s in (1, 2, 3)])

    whole, chunk = (16, 2, 256, 128), sds((256, 256), BF)
    x = (me // 2) % 4
    grads = [
        lax.dynamic_slice_in_dim(grad_out, ((x + s) % 4) * 256, 256, 0) for s in range(4)
    ]
    grads = [grads[0]] + [shift_x(grads[s], s) for s in (1, 2, 3)]
    act, slope = call(
        first_body,
        [sds(whole, BF), sds((4, 2, 256, 128), F32)],
        [tokens, w_first],
        67_000_000 * 2,
        3_500_000,
    )
    act, *_ = lax.optimization_barrier((act, w0, *grads[1:]))
    mine = exchange(act)
    weights = [w_own, w0] + [shift_z(w0, t) for t in (1, 2, 3)]

    inputs = [*weights, *grads]
    away, own = pl.pallas_call(
        back_body,
        out_shape=[sds(whole, BF)] * 2,
        in_specs=[pl.BlockSpec(memory_space=pltpu.SMEM)] * 3 + [pl.BlockSpec(memory_space=pl.ANY)] * 9,
        out_specs=[pl.BlockSpec(memory_space=pltpu.VMEM)] * 2,
        scratch_shapes=[pltpu.VMEM(part.shape, BF) for part in inputs]
        + [pltpu.VMEM((64, 256, 128), F32), pltpu.SemaphoreType.DMA((9,))],
        compiler_params=pltpu.CompilerParams(vmem_limit_bytes=LIMIT),
        cost_estimate=pl.CostEstimate(flops=1_080_000_000, bytes_accessed=9_000_000, transcendentals=0),
    )(pos, tile_src, tile_live, *inputs)
    away, mine = lax.optimization_barrier((away, mine))
    parts = (own.astype(F32) + swap_core(away).astype(F32)).astype(BF)
    parts, mine_later = lax.optimization_barrier((parts, mine))
    sums = exchange(parts)
    other = swap_core(mine_later)

    slab = (8, 8, 32, 128)
    cat = pltpu.VMEM((2, 256, 1024), BF)
    abuf = pltpu.VMEM((2, 16, 2, 256, 128), BF)
    parts = call(
        weight_body,
        [sds(slab, F32)] + [sds(slab, BF)] * 3,
        [pos, tile_src, tile_live, mine, other, *grads],
        540_000_000 * 2,
        12_000_000,
        [abuf, cat, pltpu.VMEM((2, 8, 128, 128), F32), pltpu.SemaphoreType.DMA((2,))],
        (3, 4),
    )
    summed, after_z = parts[0], [shift_z(parts[t], t) for t in (1, 2, 3)]
    other, _ = lax.optimization_barrier((other, parts[1]))
    layer = call(
        layer_body,
        [chunk] * 4,
        [pos, tile_src, tile_live, *weights, mine, other],
        540_000_000 * 2,
        9_000_000,
        [abuf, cat, pltpu.SemaphoreType.DMA((2,))],
        (8, 9),
    )
    rows = [layer[0], shift_x(layer[1], -1), None, shift_x(layer[3], -3)]
    layer2, _ = lax.optimization_barrier((layer[2], rows[1]))
    rows[2] = shift_x(layer2, -2)
    sums, *_ = lax.optimization_barrier((sums, layer[2], rows[1], rows[3], layer2))
    outs = call(
        last_body,
        [sds((1024, 256), BF)] + [sds((2, 32, 128), F32)] * 4,
        [pos, tokens, w_first, slope, sums],
        2 * 67_000_000 * 2,
        3_500_000,
        [pltpu.VMEM((2, 128, 128), F32)],
    )
    grad_tokens = outs[0]
    grad_first = outs[1]
    for part in [shift_z(outs[1 + t], t) for t in (1, 2, 3)]:
        grad_first = grad_first + part
    for part in after_z:
        summed = summed + part.astype(F32)
    grad_second = summed[0:2]
    for part in [shift_x(summed[2 * s : 2 * s + 2].astype(BF), -s) for s in (1, 2, 3)]:
        grad_second = grad_second + part.astype(F32)

    (layer_out,) = call(join_body, [sds((1024, 256), BF)], [pos, *rows], 0, 1_000_000)
    return (layer_out, grad_tokens, grad_first, grad_second)


def solution(mesh):
    in_specs = (
        P("tok", "blk"),
        P("blk", None, None),
        P("blk", None, None, None),
        P(),
        P(),
        P("tok", "blk"),
    )
    out_specs = (
        P("tok", "blk"),
        P("tok", "blk"),
        P("blk", "tok", None),
        P("blk", None, "tok", None),
    )
    return jax.shard_map(shards, mesh=mesh, in_specs=in_specs, out_specs=out_specs, check_vma=False)
```

```python
import functools

import jax
import jax.numpy as jnp
from jax import lax
from jax.experimental import pallas as pl
from jax.experimental.pallas import tpu as pltpu
from jax.sharding import PartitionSpec as P

NY, NX, NC, NZ = 4, 4, 2, 4
BF, F32 = jnp.bfloat16, jnp.float32
LIMIT = 56 * 1024 * 1024
ROOT = 0.7978845608028654
CUBE = 0.044715
def along(dy, dx, dc):
    pairs = []
    for y in range(NY):
        for x in range(NX):
            for c in range(NC):
                to = (((y + dy) % NY) * NX + (x + dx) % NX) * NC + (c + dc) % NC
                pairs.append(((y * NX + x) * NC + c, to))
    return pairs


def shift_x(value, step):
    return lax.ppermute(value, "blk", along(0, step, 0))


def swap_core(value):
    return lax.ppermute(value, "blk", along(0, 0, 1))


def shift_z(value, step):
    return lax.ppermute(value, "tok", [(z, (z + step) % NZ) for z in range(NZ)])


def dot(a, b, ca, cb):
    return lax.dot_general(a, b, (((ca,), (cb,)), ((), ())), preferred_element_type=F32)


def window(value):
    return pl.BlockSpec(value.shape, lambda step: (0,) * len(value.shape))


def call(body, outs, args, flops, nbytes, scratch=(), kept=()):
    specs = []
    for n, arg in enumerate(args):
        if arg.dtype == jnp.int32:
            specs.append(pl.BlockSpec(memory_space=pltpu.SMEM))
        elif n in kept:
            specs.append(pl.BlockSpec(memory_space=pl.ANY))
        else:
            specs.append(window(arg))
    return pl.pallas_call(
        lambda *refs: body(*refs),
        grid=(1,),
        out_shape=outs,
        in_specs=specs,
        out_specs=[window(out) for out in outs],
        scratch_shapes=list(scratch),
        compiler_params=pltpu.CompilerParams(vmem_limit_bytes=LIMIT),
        cost_estimate=pl.CostEstimate(flops=flops, bytes_accessed=nbytes, transcendentals=0),
    )(*args)


def sds(shape, dtype):
    return jax.ShapeDtypeStruct(shape, dtype)


def first_body(tok, wf, act, slope):
    for n in range(4):
        for p in range(2):
            pre = dot(tok[n * 256 : (n + 1) * 256, p * 128 : (p + 1) * 128], wf[p], 1, 0)
            sq = pre * pre
            th = jnp.tanh(ROOT * pre * (1.0 + CUBE * sq))
            out = (0.5 * pre * (1.0 + th)).astype(BF)
            for y in range(4):
                act[y * 4 + n, p] = out
            slope[n, p] = 0.5 * (1.0 + th) + 0.5 * pre * (1.0 - th * th) * (
                ROOT * (1.0 + 3.0 * CUBE * sq)
            )


def tiles(s, p, z, w_own, parts):
    found = []
    for t in range(4):
        for kk in range(2):
            rows = slice(kk * 128, (kk + 1) * 128)
            if s == 0:
                k = 2 * t + kk
                found.append((k, w_own, (p, slice(k * 128, (k + 1) * 128))))
            else:
                found.append((((z - t) & 3) * 2 + kk, parts[t], (s - 1, p, rows)))
    return found


def back_body(pos, src, live, *refs):
    away, own = refs[9:11], refs[11:13]
    w_own, w0, w1, w2, w3, g0, g1, g2, g3 = refs[13:22]
    acc, sems = refs[22:]
    copies = [pltpu.make_async_copy(refs[n], refs[13 + n], sems.at[n]) for n in range(9)]
    for n in (0, 5, 1, 2, 3, 4, 6, 7, 8):
        copies[n].start()
    y, x, c, z = pos[0], pos[1], pos[2], pos[3]
    acc[...] = jnp.zeros_like(acc)
    for s, g in enumerate((g0, g1, g2, g3)):
        for n in ((0, 5), (1, 2, 3, 4, 6), (7,), (8,))[s]:
            copies[n].wait()
        for p in range(2):
            block = ((y * 4 + ((x - s) & 3)) * 2 + c) * 2 + p
            grad = g[:, p * 128 : (p + 1) * 128]
            for slot, ref, at in tiles(s, p, z, w_own, (w0, w1, w2, w3)):
                j = src[block, slot]
                scale = live[block, slot].astype(F32)
                r = j >> 1
                acc[((r & 1) ^ c) * 32 + (r >> 1) * 2 + (j & 1)] += dot(grad, ref[at], 1, 1) * scale
    for n in range(16):
        away[n // 8][n % 8] = acc[32 + 2 * n : 34 + 2 * n].astype(BF)
        own[n // 8][n % 8] = acc[2 * n : 2 * n + 2].astype(BF)


def load_acts(mine, other, abuf, sems):
    copies = [
        pltpu.make_async_copy(part, abuf.at[n], sems.at[n]) for n, part in enumerate((mine, other))
    ]
    for copy in copies:
        copy.start()
    for copy in copies:
        copy.wait()


def pick(cat, n, at, abuf, src, live, block, slot, c):
    j = src[block, slot]
    scale = live[block, slot].astype(F32).astype(BF)
    r = j >> 1
    cat[n, :, at * 128 : (at + 1) * 128] = abuf[(r & 1) ^ c, r >> 1, j & 1] * scale


def weight_body(pos, src, live, mine, other, g0, g1, g2, g3, z0, z1, z2, z3, abuf, cat, grads, sems):
    y, x, c, z = pos[0], pos[1], pos[2], pos[3]
    load_acts(mine, other, abuf, sems)
    for s, g in enumerate((g0, g1, g2, g3)):
        for p in range(2):
            n = s * 2 + p
            block = ((y * 4 + ((x - s) & 3)) * 2 + c) * 2 + p
            for k in range(8):
                pick(cat, p, k, abuf, src, live, block, k, c)
            grads[p] = dot(cat[p], g[:, p * 128 : (p + 1) * 128], 0, 0).reshape(8, 128, 128)
            for t, to in enumerate((z0, z1, z2, z3)):
                rows = pl.ds(pl.multiple_of(((z + t) & 3) * 32, 32), 32)
                to[n] = grads[p, :, rows, :].astype(to.dtype)


def layer_body(pos, src, live, w_own, w0, w1, w2, w3, mine, other, l0, l1, l2, l3, abuf, cat, sems):
    y, x, c, z = pos[0], pos[1], pos[2], pos[3]
    load_acts(mine, other, abuf, sems)
    for s, out in enumerate((l0, l1, l2, l3)):
        for p in range(2):
            block = ((y * 4 + ((x - s) & 3)) * 2 + c) * 2 + p
            found = tiles(s, p, z, w_own, (w0, w1, w2, w3))
            for k, (slot, _, _) in enumerate(found):
                pick(cat, p, k, abuf, src, live, block, slot, c)
            total = None
            for k in range(0, 8, 2):
                _, ref, at = found[k]
                both = ref[at[:-1] + (slice(at[-1].start, at[-1].start + 256),)]
                part = dot(cat[p, :, k * 128 : (k + 2) * 128], both, 1, 0)
                total = part if total is None else total + part
            out[:, p * 128 : (p + 1) * 128] = total.astype(BF)


def join_body(pos, p0, p1, p2, p3, out):
    x = pos[1]
    for s, part in enumerate((p0, p1, p2, p3)):
        out[pl.ds(pl.multiple_of(((x + s) & 3) * 256, 256), 256), :] = part[...]


def last_body(pos, tok, wf, slope, sums, gt, f0, f1, f2, f3, total):
    z = pos[3]
    for n in range(4):
        rows = slice(n * 256, (n + 1) * 256)
        for p in range(2):
            cols = slice(p * 128, (p + 1) * 128)
            grad_act = sums[n, p].astype(F32)
            for y in range(1, 4):
                grad_act += sums[y * 4 + n, p].astype(F32)
            grad_pre = (grad_act * slope[n, p]).astype(BF)
            gt[rows, cols] = dot(grad_pre, wf[p], 1, 1).astype(BF)
            part = dot(tok[rows, cols], grad_pre, 0, 0)
            if n == 0:
                total[p] = part
            else:
                total[p] += part
    for t, out in enumerate((f0, f1, f2, f3)):
        out[...] = total[:, pl.ds(pl.multiple_of(((z + t) & 3) * 32, 32), 32), :]


def exchange(value):
    groups = [[n * NC + c for n in range(NY * NX)] for c in range(NC)]
    return lax.all_to_all(value, "blk", 0, 0, axis_index_groups=groups, tiled=True)


def shards(tokens, w_first, w_second, tile_src, tile_live, grad_out):
    me, z = lax.axis_index("blk"), lax.axis_index("tok")
    pos = jnp.stack([me // 8, (me // 2) % 4, me % 2, z]).astype(jnp.int32)
    w_own = w_second.reshape(2, 1024, 128)

    quarter = lax.dynamic_slice_in_dim(w_own, z * 256, 256, 1)
    w0 = jnp.stack([shift_x(quarter, s) for s in (1, 2, 3)])

    whole, chunk = (16, 2, 256, 128), sds((256, 256), BF)
    x = (me // 2) % 4
    grads = [
        lax.dynamic_slice_in_dim(grad_out, ((x + s) % 4) * 256, 256, 0) for s in range(4)
    ]
    grads = [grads[0]] + [shift_x(grads[s], s) for s in (1, 2, 3)]
    act, slope = call(
        first_body,
        [sds(whole, BF), sds((4, 2, 256, 128), F32)],
        [tokens, w_first],
        67_000_000 * 2,
        3_500_000,
    )
    act, *_ = lax.optimization_barrier((act, w0, *grads[1:]))
    mine = exchange(act)
    weights = [w_own, w0] + [shift_z(w0, t) for t in (1, 2, 3)]

    inputs = [*weights, *grads]
    half = sds((8, 2, 256, 128), BF)
    *away, own_low, own_high = pl.pallas_call(
        back_body,
        out_shape=[half] * 4,
        in_specs=[pl.BlockSpec(memory_space=pltpu.SMEM)] * 3 + [pl.BlockSpec(memory_space=pl.ANY)] * 9,
        out_specs=[pl.BlockSpec(memory_space=pltpu.VMEM)] * 4,
        scratch_shapes=[pltpu.VMEM(part.shape, BF) for part in inputs]
        + [pltpu.VMEM((64, 256, 128), F32), pltpu.SemaphoreType.DMA((9,))],
        compiler_params=pltpu.CompilerParams(vmem_limit_bytes=LIMIT),
        cost_estimate=pl.CostEstimate(flops=1_080_000_000, bytes_accessed=9_000_000, transcendentals=0),
    )(pos, tile_src, tile_live, *inputs)
    *away, mine = lax.optimization_barrier((*away, mine))
    parts = jnp.concatenate(
        [
            (own.astype(F32) + swap_core(part).astype(F32)).astype(BF)
            for own, part in zip((own_low, own_high), away)
        ]
    )
    parts, mine_later = lax.optimization_barrier((parts, mine))
    sums = exchange(parts)
    other = swap_core(mine_later)

    slab = (8, 8, 32, 128)
    cat = pltpu.VMEM((2, 256, 1024), BF)
    abuf = pltpu.VMEM((2, 16, 2, 256, 128), BF)
    parts = call(
        weight_body,
        [sds(slab, F32)] + [sds(slab, BF)] * 3,
        [pos, tile_src, tile_live, mine, other, *grads],
        540_000_000 * 2,
        12_000_000,
        [abuf, cat, pltpu.VMEM((2, 8, 128, 128), F32), pltpu.SemaphoreType.DMA((2,))],
        (3, 4),
    )
    summed, after_z = parts[0], [shift_z(parts[t], t) for t in (1, 2, 3)]
    other, _ = lax.optimization_barrier((other, parts[1]))
    layer = call(
        layer_body,
        [chunk] * 4,
        [pos, tile_src, tile_live, *weights, mine, other],
        540_000_000 * 2,
        9_000_000,
        [abuf, cat, pltpu.SemaphoreType.DMA((2,))],
        (8, 9),
    )
    rows = [layer[0], shift_x(layer[1], -1), None, shift_x(layer[3], -3)]
    layer2, _ = lax.optimization_barrier((layer[2], rows[1]))
    rows[2] = shift_x(layer2, -2)
    sums, *_ = lax.optimization_barrier((sums, layer[2], rows[1], rows[3], layer2))
    outs = call(
        last_body,
        [sds((1024, 256), BF)] + [sds((2, 32, 128), F32)] * 4,
        [pos, tokens, w_first, slope, sums],
        2 * 67_000_000 * 2,
        3_500_000,
        [pltpu.VMEM((2, 128, 128), F32)],
    )
    grad_tokens = outs[0]
    grad_first = outs[1]
    for part in [shift_z(outs[1 + t], t) for t in (1, 2, 3)]:
        grad_first = grad_first + part
    for part in after_z:
        summed = summed + part.astype(F32)
    grad_second = summed[0:2]
    for part in [shift_x(summed[2 * s : 2 * s + 2].astype(BF), -s) for s in (1, 2, 3)]:
        grad_second = grad_second + part.astype(F32)

    (layer_out,) = call(join_body, [sds((1024, 256), BF)], [pos, *rows], 0, 1_000_000)
    return (layer_out, grad_tokens, grad_first, grad_second)


def solution(mesh):
    in_specs = (
        P("tok", "blk"),
        P("blk", None, None),
        P("blk", None, None, None),
        P(),
        P(),
        P("tok", "blk"),
    )
    out_specs = (
        P("tok", "blk"),
        P("tok", "blk"),
        P("blk", "tok", None),
        P("blk", None, "tok", None),
    )
    return jax.shard_map(shards, mesh=mesh, in_specs=in_specs, out_specs=out_specs, check_vma=False)
```

```python
import functools

import jax
import jax.numpy as jnp
from jax import lax
from jax.experimental import pallas as pl
from jax.experimental.pallas import tpu as pltpu
from jax.sharding import PartitionSpec as P

NY, NX, NC, NZ = 4, 4, 2, 4
BF, F32 = jnp.bfloat16, jnp.float32
LIMIT = 56 * 1024 * 1024
ROOT = 0.7978845608028654
CUBE = 0.044715
def along(dy, dx, dc):
    pairs = []
    for y in range(NY):
        for x in range(NX):
            for c in range(NC):
                to = (((y + dy) % NY) * NX + (x + dx) % NX) * NC + (c + dc) % NC
                pairs.append(((y * NX + x) * NC + c, to))
    return pairs


def shift_x(value, step):
    return lax.ppermute(value, "blk", along(0, step, 0))


def swap_core(value):
    return lax.ppermute(value, "blk", along(0, 0, 1))


def shift_z(value, step):
    return lax.ppermute(value, "tok", [(z, (z + step) % NZ) for z in range(NZ)])


def dot(a, b, ca, cb):
    return lax.dot_general(a, b, (((ca,), (cb,)), ((), ())), preferred_element_type=F32)


def window(value):
    return pl.BlockSpec(value.shape, lambda step: (0,) * len(value.shape))


def call(body, outs, args, flops, nbytes, scratch=(), kept=()):
    specs = []
    for n, arg in enumerate(args):
        if arg.dtype == jnp.int32:
            specs.append(pl.BlockSpec(memory_space=pltpu.SMEM))
        elif n in kept:
            specs.append(pl.BlockSpec(memory_space=pl.ANY))
        else:
            specs.append(window(arg))
    return pl.pallas_call(
        lambda *refs: body(*refs),
        grid=(1,),
        out_shape=outs,
        in_specs=specs,
        out_specs=[window(out) for out in outs],
        scratch_shapes=list(scratch),
        compiler_params=pltpu.CompilerParams(vmem_limit_bytes=LIMIT),
        cost_estimate=pl.CostEstimate(flops=flops, bytes_accessed=nbytes, transcendentals=0),
    )(*args)


def sds(shape, dtype):
    return jax.ShapeDtypeStruct(shape, dtype)


def first_body(tok, wf, act, slope):
    for n in range(4):
        for p in range(2):
            pre = dot(tok[n * 256 : (n + 1) * 256, p * 128 : (p + 1) * 128], wf[p], 1, 0)
            sq = pre * pre
            th = jnp.tanh(ROOT * pre * (1.0 + CUBE * sq))
            out = (0.5 * pre * (1.0 + th)).astype(BF)
            for y in range(4):
                act[y * 4 + n, p] = out
            slope[n, p] = 0.5 * (1.0 + th) + 0.5 * pre * (1.0 - th * th) * (
                ROOT * (1.0 + 3.0 * CUBE * sq)
            )


def tiles(s, p, z, w_own, parts):
    found = []
    for t in range(4):
        for kk in range(2):
            rows = slice(kk * 128, (kk + 1) * 128)
            if s == 0:
                k = 2 * t + kk
                found.append((k, w_own, (p, slice(k * 128, (k + 1) * 128))))
            else:
                found.append((((z - t) & 3) * 2 + kk, parts[t], (s - 1, p, rows)))
    return found


def back_body(pos, src, live, *refs):
    away, own = refs[9:11], refs[11:13]
    w_own, w0, w1, w2, w3, g0, g1, g2, g3 = refs[13:22]
    acc, sems = refs[22:]
    copies = [pltpu.make_async_copy(refs[n], refs[13 + n], sems.at[n]) for n in range(9)]
    for n in (0, 5, 1, 2, 3, 4, 6, 7, 8):
        copies[n].start()
    y, x, c, z = pos[0], pos[1], pos[2], pos[3]
    acc[...] = jnp.zeros_like(acc)
    for s, g in enumerate((g0, g1, g2, g3)):
        for n in ((0, 5), (1, 2, 3, 4, 6), (7,), (8,))[s]:
            copies[n].wait()
        for p in range(2):
            block = ((y * 4 + ((x - s) & 3)) * 2 + c) * 2 + p
            grad = g[:, p * 128 : (p + 1) * 128]
            for slot, ref, at in tiles(s, p, z, w_own, (w0, w1, w2, w3)):
                j = src[block, slot]
                scale = live[block, slot].astype(F32)
                r = j >> 1
                acc[((r & 1) ^ c) * 32 + (r >> 1) * 2 + (j & 1)] += dot(grad, ref[at], 1, 1) * scale
    for n in range(16):
        away[n // 8][n % 8] = acc[32 + 2 * n : 34 + 2 * n].astype(BF)
        own[n // 8][n % 8] = acc[2 * n : 2 * n + 2].astype(BF)


def load_acts(mine, other, abuf, sems):
    copies = [
        pltpu.make_async_copy(part, abuf.at[n], sems.at[n]) for n, part in enumerate((mine, other))
    ]
    for copy in copies:
        copy.start()
    for copy in copies:
        copy.wait()


def pick(cat, n, at, abuf, src, live, block, slot, c):
    j = src[block, slot]
    scale = live[block, slot].astype(F32).astype(BF)
    r = j >> 1
    cat[n, :, at * 128 : (at + 1) * 128] = abuf[(r & 1) ^ c, r >> 1, j & 1] * scale


def weight_body(pos, src, live, mine, other, g0, g1, g2, g3, z0, z1, z2, z3, abuf, cat, grads, sems):
    y, x, c, z = pos[0], pos[1], pos[2], pos[3]
    load_acts(mine, other, abuf, sems)
    for s, g in enumerate((g0, g1, g2, g3)):
        for p in range(2):
            n = s * 2 + p
            block = ((y * 4 + ((x - s) & 3)) * 2 + c) * 2 + p
            for k in range(8):
                pick(cat, p, k, abuf, src, live, block, k, c)
            grads[p] = dot(cat[p], g[:, p * 128 : (p + 1) * 128], 0, 0).reshape(8, 128, 128)
            for t, to in enumerate((z0, z1, z2, z3)):
                rows = pl.ds(pl.multiple_of(((z + t) & 3) * 32, 32), 32)
                to[n] = grads[p, :, rows, :].astype(to.dtype)


def layer_body(pos, src, live, w_own, w0, w1, w2, w3, mine, other, l0, l1, l2, l3, abuf, cat, sems):
    y, x, c, z = pos[0], pos[1], pos[2], pos[3]
    load_acts(mine, other, abuf, sems)
    for s, out in enumerate((l0, l1, l2, l3)):
        for p in range(2):
            block = ((y * 4 + ((x - s) & 3)) * 2 + c) * 2 + p
            found = tiles(s, p, z, w_own, (w0, w1, w2, w3))
            for k, (slot, _, _) in enumerate(found):
                pick(cat, p, k, abuf, src, live, block, slot, c)
            total = None
            for k in range(0, 8, 2):
                _, ref, at = found[k]
                both = ref[at[:-1] + (slice(at[-1].start, at[-1].start + 256),)]
                part = dot(cat[p, :, k * 128 : (k + 2) * 128], both, 1, 0)
                total = part if total is None else total + part
            out[:, p * 128 : (p + 1) * 128] = total.astype(BF)


def join_body(pos, p0, p1, p2, p3, out):
    x = pos[1]
    for s, part in enumerate((p0, p1, p2, p3)):
        out[pl.ds(pl.multiple_of(((x + s) & 3) * 256, 256), 256), :] = part[...]


def last_body(pos, tok, wf, slope, sums, gt, f0, f1, f2, f3, total):
    z = pos[3]
    for n in range(4):
        rows = slice(n * 256, (n + 1) * 256)
        for p in range(2):
            cols = slice(p * 128, (p + 1) * 128)
            grad_act = sums[n, p].astype(F32)
            for y in range(1, 4):
                grad_act += sums[y * 4 + n, p].astype(F32)
            grad_pre = (grad_act * slope[n, p]).astype(BF)
            gt[rows, cols] = dot(grad_pre, wf[p], 1, 1).astype(BF)
            part = dot(tok[rows, cols], grad_pre, 0, 0)
            if n == 0:
                total[p] = part
            else:
                total[p] += part
    for t, out in enumerate((f0, f1, f2, f3)):
        out[...] = total[:, pl.ds(pl.multiple_of(((z + t) & 3) * 32, 32), 32), :]


def exchange(value):
    groups = [[n * NC + c for n in range(NY * NX)] for c in range(NC)]
    return lax.all_to_all(value, "blk", 0, 0, axis_index_groups=groups, tiled=True)


def shards(tokens, w_first, w_second, tile_src, tile_live, grad_out):
    me, z = lax.axis_index("blk"), lax.axis_index("tok")
    pos = jnp.stack([me // 8, (me // 2) % 4, me % 2, z]).astype(jnp.int32)
    w_own = w_second.reshape(2, 1024, 128)

    quarter = lax.dynamic_slice_in_dim(w_own, z * 256, 256, 1)
    w0 = jnp.stack([shift_x(quarter, s) for s in (1, 2, 3)])

    whole, chunk = (16, 2, 256, 128), sds((256, 256), BF)
    x = (me // 2) % 4
    grads = [
        lax.dynamic_slice_in_dim(grad_out, ((x + s) % 4) * 256, 256, 0) for s in range(4)
    ]
    grads = [grads[0]] + [shift_x(grads[s], s) for s in (1, 2, 3)]
    act, slope = call(
        first_body,
        [sds(whole, BF), sds((4, 2, 256, 128), F32)],
        [tokens, w_first],
        67_000_000 * 2,
        3_500_000,
    )
    act, *_ = lax.optimization_barrier((act, w0, *grads[1:]))
    mine_ready = act
    mine = exchange(act)
    weights = [w_own, w0] + [shift_z(w0, t) for t in (1, 2, 3)]
    grad_later, _ = lax.optimization_barrier((grad_out, mine_ready))
    grads[0] = lax.dynamic_slice_in_dim(grad_later, x * 256, 256, 0)

    inputs = [*weights, *grads]
    half = sds((8, 2, 256, 128), BF)
    *away, own_low, own_high = pl.pallas_call(
        back_body,
        out_shape=[half] * 4,
        in_specs=[pl.BlockSpec(memory_space=pltpu.SMEM)] * 3 + [pl.BlockSpec(memory_space=pl.ANY)] * 9,
        out_specs=[pl.BlockSpec(memory_space=pltpu.VMEM)] * 4,
        scratch_shapes=[pltpu.VMEM(part.shape, BF) for part in inputs]
        + [pltpu.VMEM((64, 256, 128), F32), pltpu.SemaphoreType.DMA((9,))],
        compiler_params=pltpu.CompilerParams(vmem_limit_bytes=LIMIT),
        cost_estimate=pl.CostEstimate(flops=1_080_000_000, bytes_accessed=9_000_000, transcendentals=0),
    )(pos, tile_src, tile_live, *inputs)
    *away, mine = lax.optimization_barrier((*away, mine))
    parts = jnp.concatenate(
        [
            (own.astype(F32) + swap_core(part).astype(F32)).astype(BF)
            for own, part in zip((own_low, own_high), away)
        ]
    )
    parts, mine_later = lax.optimization_barrier((parts, mine))
    sums = exchange(parts)
    other = swap_core(mine_later)

    slab = (8, 8, 32, 128)
    cat = pltpu.VMEM((2, 256, 1024), BF)
    abuf = pltpu.VMEM((2, 16, 2, 256, 128), BF)
    parts = call(
        weight_body,
        [sds(slab, F32)] + [sds(slab, BF)] * 3,
        [pos, tile_src, tile_live, mine, other, *grads],
        540_000_000 * 2,
        12_000_000,
        [abuf, cat, pltpu.VMEM((2, 8, 128, 128), F32), pltpu.SemaphoreType.DMA((2,))],
        (3, 4),
    )
    summed, after_z = parts[0], [shift_z(parts[t], t) for t in (1, 2, 3)]
    other, _ = lax.optimization_barrier((other, parts[1]))
    layer = call(
        layer_body,
        [chunk] * 4,
        [pos, tile_src, tile_live, *weights, mine, other],
        540_000_000 * 2,
        9_000_000,
        [abuf, cat, pltpu.SemaphoreType.DMA((2,))],
        (8, 9),
    )
    rows = [layer[0], shift_x(layer[1], -1), None, shift_x(layer[3], -3)]
    layer2, _ = lax.optimization_barrier((layer[2], rows[1]))
    rows[2] = shift_x(layer2, -2)
    sums, *_ = lax.optimization_barrier((sums, layer[2], rows[1], rows[3], layer2))
    outs = call(
        last_body,
        [sds((1024, 256), BF)] + [sds((2, 32, 128), F32)] * 4,
        [pos, tokens, w_first, slope, sums],
        2 * 67_000_000 * 2,
        3_500_000,
        [pltpu.VMEM((2, 128, 128), F32)],
    )
    grad_tokens = outs[0]
    grad_first = outs[1]
    for part in [shift_z(outs[1 + t], t) for t in (1, 2, 3)]:
        grad_first = grad_first + part
    for part in after_z:
        summed = summed + part.astype(F32)
    grad_second = summed[0:2]
    for part in [shift_x(summed[2 * s : 2 * s + 2].astype(BF), -s) for s in (1, 2, 3)]:
        grad_second = grad_second + part.astype(F32)

    (layer_out,) = call(join_body, [sds((1024, 256), BF)], [pos, *rows], 0, 1_000_000)
    return (layer_out, grad_tokens, grad_first, grad_second)


def solution(mesh):
    in_specs = (
        P("tok", "blk"),
        P("blk", None, None),
        P("blk", None, None, None),
        P(),
        P(),
        P("tok", "blk"),
    )
    out_specs = (
        P("tok", "blk"),
        P("tok", "blk"),
        P("blk", "tok", None),
        P("blk", None, "tok", None),
    )
    return jax.shard_map(shards, mesh=mesh, in_specs=in_specs, out_specs=out_specs, check_vma=False)
```
